32 devices in a mesh: lat: 8 (over y, x, core), lon: 4 (over z).
Axes of the slice: x: 2, y: 2, z: 4, core: 2. Of those that a mesh axis runs over, the one named last changes fastest.
Arguments:
- initial: float32 [64, 128, 512], P(None, 'lat', 'lon'), may hold values from -6 to 6
- east_wind: float32 [64, 128, 512], P(None, 'lat', 'lon'), may hold values from -2.5 to 2.5
- north_wind: float32 [64, 128, 512], P(None, 'lat', 'lon'), may hold values from -2.5 to 2.5
- east_mask: int32 [64, 128, 512], P(None, 'lat', 'lon'), may hold values from 0 to 1
- north_mask: int32 [64, 128, 512], P(None, 'lat', 'lon'), may hold values from 0 to 1
- mixing: float32 [63], replicated, may hold values from 0.02 to 0.2
- obs_cell: int32 [8, 4, 4, 256], P('lat', 'lon'), may hold values from 0 to 2047
- obs_level: int32 [8, 4, 4, 256], P('lat', 'lon'), may hold values from 0 to 63
- obs_value: float32 [8, 4, 4, 256], P('lat', 'lon'), may hold values from -6 to 6
- obs_weight: float32 [8, 4, 4, 256], P('lat', 'lon'), may hold values from 0.2 to 2
Outputs:
- gradient: float32 [64, 128, 512], P(None, 'lat', 'lon')
- cost: float32 [], replicated
The draws below stay inside these ranges and needn't reach their ends.
Inputs may be any that keep to these rules, and one draw needn't show every extreme that they name: `obs_cell`: row times 128 plus column within the block.
All inputs are finite; a program needn't handle non-finite values.
Results may differ from the reference program's by a relative error of at most 0.0003.
Values sent between devices are 32-bit elements; how exact they have to be, the bound alone decides.
A program may use at most 64 MiB of HBM per device.

```python
import math
import jax
import jax.numpy as jnp

L = 64
CLAT = 16
CLON = 128
STEPS = 4
NOBS = 256
NY = 128
NX = 512
N_LAT = 8
N_LON = 4


def with_ends(entries, own_key, least, high):
    longest = entries.shape.index(max(entries.shape))
    spots = []
    for shift in (0, 1):
        where = [jax.random.randint(jax.random.fold_in(own_key, axis), (), 0, length) for axis, length in enumerate(entries.shape)]
        where[longest] = (where[longest] + shift) % entries.shape[longest]
        spots.append(tuple(where))
    return entries.at[spots[0]].set(least).at[spots[1]].set(high)


def shard_levels(stream_key, extent, shards, least, high):
    level = 1.0
    for dim, shards_of in shards:
        draws = jax.random.uniform(jax.random.fold_in(jax.random.fold_in(stream_key, 6), dim), (shards_of,), jnp.float32, least / len(shards), high / len(shards))
        level = level * jnp.repeat(jnp.exp(draws), extent[dim] // shards_of).reshape((-1,) + (1,) * (len(extent) - 1 - dim))
    return level


def normal_values(rng, shape, deviation, limit, shards=(), held_as=jnp.bfloat16):
    values = deviation * jax.random.normal(rng, shape, jnp.float32)
    if shards:
        values = values * shard_levels(rng, shape, shards, -0.22, 0.18)
    return jnp.clip(values, -limit, limit).astype(held_as)


def setup_inputs(seed: int = 0) -> dict:
    keys = jax.random.split(jax.random.key(seed), 11)
    return {
        "initial": normal_values(keys[0], (L, NY, NX), 1.0, 6.0, ((1, 8), (2, 4)), jnp.float32),
        "east_wind": normal_values(keys[1], (L, NY, NX), 0.2, 2.5, ((1, 8), (2, 4)), jnp.float32),
        "north_wind": normal_values(keys[2], (L, NY, NX), 0.2, 2.5, ((1, 8), (2, 4)), jnp.float32),
        "east_mask": with_ends(jax.random.randint(keys[3], (L, NY, NX), 0, 2), jax.random.fold_in(keys[3], 1), 0, 1).astype(jnp.int32),
        "north_mask": with_ends(jax.random.randint(keys[4], (L, NY, NX), 0, 2), jax.random.fold_in(keys[4], 1), 0, 1).astype(jnp.int32),
        "mixing": jnp.clip(jnp.exp(jax.random.uniform(keys[5], (L - 1,), jnp.float32, math.log(0.02), math.log(0.2))), 0.02, 0.2),
        "obs_cell": with_ends(jax.random.randint(keys[6], (N_LAT, N_LON, STEPS, NOBS), 0, CLAT * CLON), jax.random.fold_in(keys[6], 1), 0, (CLAT * CLON) - 1).astype(jnp.int32),
        "obs_level": with_ends(jax.random.randint(keys[7], (N_LAT, N_LON, STEPS, NOBS), 0, L), jax.random.fold_in(keys[7], 1), 0, L - 1).astype(jnp.int32),
        "obs_value": normal_values(keys[8], (N_LAT, N_LON, STEPS, NOBS), 1.0, 6.0, ((0, 8), (1, 4)), jnp.float32),
        "obs_weight": jnp.clip(jnp.exp(math.log(2.0) - 2.3025851 * jax.random.uniform(keys[9], (N_LAT, N_LON, STEPS, NOBS), jnp.float32) ** shard_levels(keys[9], (N_LAT, N_LON, STEPS, NOBS), ((0, 8), (1, 4)), -0.2, 0.2)), 0.2, 2.0),
    }


def face_parts(velocity, branch):
    share = jnp.where(branch == 1, jnp.where(velocity > 0, 1.0, 0.0), 0.5)
    return (velocity * share, velocity * (1.0 - share))

def vertical(field, mixing):
    flux = mixing[:, None, None] * (field[1:] - field[:-1])
    zero_row = jnp.zeros_like(field[:1])
    return jnp.concatenate([flux, zero_row], 0) - jnp.concatenate([zero_row, flux], 0)

def reference(initial, east_wind, north_wind, east_mask, north_mask, mixing, obs_cell, obs_level, obs_value, obs_weight):
    west_p, west_q = face_parts(east_wind, east_mask)
    south_p, south_q = face_parts(north_wind, north_mask)
    keep = (jnp.arange(NY) > 0)[None, :, None]
    south_p = jnp.where(keep, south_p, 0.0)
    south_q = jnp.where(keep, south_q, 0.0)
    east_p = jnp.roll(west_p, -1, 2)
    east_q = jnp.roll(west_q, -1, 2)
    zero_line = jnp.zeros_like(south_p[:, :1])
    north_p = jnp.concatenate([south_p[:, 1:], zero_line], 1)
    north_q = jnp.concatenate([south_q[:, 1:], zero_line], 1)

    def advance(field):
        west = jnp.roll(field, 1, 2)
        east = jnp.roll(field, -1, 2)
        blank = jnp.zeros_like(field[:, :1])
        south = jnp.concatenate([blank, field[:, :-1]], 1)
        north = jnp.concatenate([field[:, 1:], blank], 1)
        div_lon = east_p * field + east_q * east - west_p * west - west_q * field
        div_lat = north_p * field + north_q * north - south_p * south - south_q * field
        return field + vertical(field, mixing) - div_lon - div_lat
    flat = (obs_level * (CLAT * CLON) + obs_cell).astype(jnp.int32)
    lat_ids = jnp.arange(N_LAT)[:, None, None]
    lon_ids = jnp.arange(N_LON)[None, :, None]

    def misfit(start):
        state = start
        total = jnp.zeros((), jnp.float32)
        for step in range(STEPS):
            state = advance(state)
            blocks = state.reshape(L, N_LAT, CLAT, N_LON, CLON).transpose(1, 3, 0, 2, 4).reshape(N_LAT, N_LON, L * CLAT * CLON)
            picked = blocks[lat_ids, lon_ids, flat[:, :, step]]
            innovation = picked - obs_value[:, :, step]
            total = total + 0.5 * jnp.sum(obs_weight[:, :, step] * innovation * innovation)
        return total
    cost, pull = jax.vjp(misfit, initial)
    gradient = pull(jnp.ones_like(cost))[0]
    return (gradient, cost)
```

```python
import functools

import jax
import jax.numpy as jnp
from jax import lax
from jax.experimental import pallas as pl
from jax.experimental.pallas import tpu as pltpu
from jax.sharding import PartitionSpec as P

STEPS = 4
MESH = pl.DeviceIdType.MESH


def halves(value):
    top = value.astype(jnp.bfloat16)
    return top, (value - top.astype(jnp.float32)).astype(jnp.bfloat16)


def window(
    n_lat, n_lon, levels, rows, cols,
    start_ref, ew_ref, nw_ref, em_ref, nm_ref, mix_ref,
    cell_ref, level_ref, value_ref, weight_ref,
    grad_ref, cost_ref,
    field, source, diag, west_p, west_q, east_p, east_q, south_p, south_q,
    up, down, edge_row, edge_col, packed, face_out, face_in, cost_lon, cost_lat,
    send_sem, recv_sem, face_send, face_recv, lon_send, lon_recv, lat_send, lat_recv,
):
    la, lo = lax.axis_index("lat"), lax.axis_index("lon")
    north = (lax.rem(la + 1, n_lat), lo)
    south = (lax.rem(la + n_lat - 1, n_lat), lo)
    east = (la, lax.rem(lo + 1, n_lon))
    west = (la, lax.rem(lo + n_lon - 1, n_lon))
    lat_others = [(lax.rem(la + d, n_lat), lo) for d in range(1, n_lat)]
    lon_others = [(la, lax.rem(lo + d, n_lon)) for d in range(1, n_lon)]

    barrier = pltpu.get_barrier_semaphore()
    for other in lat_others + lon_others:
        pl.semaphore_signal(barrier, inc=1, device_id=other, device_id_type=MESH)

    lane = lax.broadcasted_iota(jnp.int32, (levels, cols), 1)
    first, last = lane == 0, lane == cols - 1

    def remote(src, dst, send, recv, target):
        return pltpu.make_async_remote_copy(
            src_ref=src, dst_ref=dst, send_sem=send, recv_sem=recv,
            device_id=target, device_id_type=MESH,
        )

    def row_copies(t):
        return (
            remote(field.at[t, 0], edge_row.at[t, 1], send_sem.at[t, 0], recv_sem.at[t, 0], south),
            remote(field.at[t, rows - 1], edge_row.at[t, 0], send_sem.at[t, 1], recv_sem.at[t, 1], north),
        )

    def col_copies(t):
        return (
            remote(packed.at[t], edge_col.at[t, 1], send_sem.at[t, 2], recv_sem.at[t, 2], west),
            remote(packed.at[t], edge_col.at[t, 0], send_sem.at[t, 3], recv_sem.at[t, 3], east),
        )

    face_copies = (
        remote(face_out, face_in, face_send.at[0], face_recv.at[0], west),
        remote(south_p.at[0], south_p.at[rows], face_send.at[1], face_recv.at[1], south),
        remote(south_q.at[0], south_q.at[rows], face_send.at[2], face_recv.at[2], south),
    )

    def pack(total, value, row):
        turned = pltpu.roll(value, 2 * row, 1)
        spot = (lane == 2 * row) | (lane == lax.rem(2 * row + cols - 1, cols))
        return jnp.where(spot, turned, total)

    def strided(ref, row):
        return ref[pl.ds(row, levels, stride=rows), :]

    def parts(wind, mask):
        share = jnp.where(mask == 1, jnp.where(wind > 0, 1.0, 0.0), 0.5)
        return wind * share, wind * (1.0 - share)

    edges = jnp.zeros((levels, cols), jnp.float32)
    faces = jnp.zeros((levels, cols), jnp.float32)
    for row in range(rows):
        value = strided(start_ref, row)
        field[0, row] = value
        edges = pack(edges, value, row)
        p, q = parts(strided(ew_ref, row), strided(em_ref, row))
        west_p[row] = p
        west_q[row] = -q
        faces = jnp.where(lane == 2 * row, pltpu.roll(p, 2 * row, 1), faces)
        faces = jnp.where(lane == 2 * row + 1, pltpu.roll(q, 2 * row + 1, 1), faces)
        p, q = parts(strided(nw_ref, row), strided(nm_ref, row))
        if row == 0:
            p = jnp.where(la > 0, p, 0.0)
            q = jnp.where(la > 0, q, 0.0)
        south_p[row] = p
        south_q[row] = -q
    packed[0] = edges
    face_out[...] = faces

    pl.semaphore_wait(barrier, n_lat + n_lon - 2)
    for copy in face_copies + row_copies(0) + col_copies(0):
        copy.start()

    up[levels - 1 : levels, :] = jnp.zeros((1, cols), jnp.float32)
    down[0:1, :] = jnp.zeros((1, cols), jnp.float32)
    for level in range(levels - 1):
        line = jnp.full((1, cols), mix_ref[level], jnp.float32)
        up[level : level + 1, :] = line
        down[level + 1 : level + 2, :] = line

    for copy in face_copies:
        copy.wait_recv()
    column = 1.0 - up[...] - down[...]
    got = face_in[...]
    for row in range(rows):
        p, q = west_p[row], west_q[row]
        turned_p = pltpu.roll(got, (cols - 2 * row) % cols, 1)
        turned_q = -pltpu.roll(got, (cols - 2 * row - 1) % cols, 1)
        p_next = pltpu.roll(jnp.where(first, turned_p, p), cols - 1, 1)
        q_next = pltpu.roll(jnp.where(first, turned_q, q), cols - 1, 1)
        east_p[row] = p_next
        east_q[row] = q_next
        diag[row] = column - q - p_next - south_q[row] - south_p[row + 1]

    def step(t, out, forward, extra, send):
        for copy in row_copies(t) + col_copies(t):
            copy.wait_recv()
        cw, ce, cs, cn = (
            (west_p, east_q, south_p, south_q) if forward else (west_q, east_p, south_q, south_p)
        )
        edge = jnp.where(lax.rem(lane, 2) == 0, edge_col[t, 1], edge_col[t, 0])

        def one(row, below, above):
            value = field[t, row]
            turned = pltpu.roll(edge, lax.rem(cols - 2 * row, cols), 1)
            at_west = pltpu.roll(jnp.where(last, turned, value), 1, 1)
            at_east = pltpu.roll(jnp.where(first, turned, value), cols - 1, 1)
            higher = pltpu.roll(value, levels - 1, 0)
            lower = pltpu.roll(value, 1, 0)
            new = (
                (diag[row] * value + cw[row] * at_west)
                + (ce[row] * at_east + cs[row] * below)
                + (cn[row + 1] * above + up[...] * higher)
                + down[...] * lower
            )
            if extra is not None:
                new = new + source[extra, pl.ds(row * levels, levels), :]
            return new

        def put(row, new):
            if out is None:
                grad_ref[pl.ds(row, levels, stride=rows), :] = new
            else:
                field[out, row] = new

        low = one(0, edge_row[t, 0], field[t, 1])
        put(0, low)
        high = one(rows - 1, field[t, rows - 2], edge_row[t, 1])
        put(rows - 1, high)
        if send:
            for copy in row_copies(out):
                copy.start()
        total = pack(pack(jnp.zeros_like(low), low, 0), high, rows - 1)

        def inner(i, total):
            for row in (1 + 2 * i, 2 + 2 * i):
                new = one(row, field[t, row - 1], field[t, row + 1])
                put(row, new)
                if send:
                    total = pack(total, new, row)
            return total

        total = lax.fori_loop(0, (rows - 2) // 2, inner, total)
        if send:
            packed[out] = total
            for copy in col_copies(out):
                copy.start()

    def observe(k, slot):
        n_obs = cell_ref.shape[1]
        cell = cell_ref[k : k + 1, :]
        place = (cell // cols) * levels + level_ref[k : k + 1, :]
        col = lax.rem(cell, cols)
        cols_hot = lax.broadcasted_iota(jnp.int32, (cols, n_obs), 0) == col
        pick = jnp.where(cols_hot, 1.0, 0.0).astype(jnp.bfloat16)

        def gather(row, total):
            top, rest = halves(field[slot, row])
            values = jnp.dot(top, pick, preferred_element_type=jnp.float32) + jnp.dot(
                rest, pick, preferred_element_type=jnp.float32
            )
            spots = lax.broadcasted_iota(jnp.int32, (levels, n_obs), 0) + row * levels
            return total + jnp.where(spots == place, values, 0.0)

        found = lax.fori_loop(0, rows, gather, jnp.zeros((levels, n_obs), jnp.float32))
        innovation = jnp.sum(found, axis=0, keepdims=True) - value_ref[k : k + 1, :]
        weighted = weight_ref[k : k + 1, :] * innovation
        top, rest = halves(weighted)
        zero = jnp.zeros((), jnp.float32)
        spread_top = jnp.where(cols_hot, top.astype(jnp.float32), zero).astype(jnp.bfloat16)
        spread_rest = jnp.where(cols_hot, rest.astype(jnp.float32), zero).astype(jnp.bfloat16)

        def scatter(row, _):
            spots = lax.broadcasted_iota(jnp.int32, (levels, n_obs), 0) + row * levels
            hot = jnp.where(spots == place, 1.0, 0.0).astype(jnp.bfloat16)
            dims = (((1,), (1,)), ((), ()))
            value = lax.dot_general(
                hot, spread_top, dims, preferred_element_type=jnp.float32
            ) + lax.dot_general(hot, spread_rest, dims, preferred_element_type=jnp.float32)
            if k == STEPS - 1:
                field[STEPS, row] = value
            else:
                source[k, pl.ds(row * levels, levels), :] = value
            return 0

        lax.fori_loop(0, rows, scatter, 0)
        return 0.5 * jnp.sum(weighted * innovation)

    cost = jnp.zeros((), jnp.float32)
    for k in range(STEPS):
        final = k == STEPS - 1
        slot = 2 * STEPS if final else k + 1
        step(k, slot, True, None, not final)
        cost = cost + observe(k, slot)

    for copy in row_copies(STEPS):
        copy.start()
    total = jnp.zeros((levels, cols), jnp.float32)
    for row in range(rows):
        total = pack(total, field[STEPS, row], row)
    packed[STEPS] = total
    for copy in col_copies(STEPS):
        copy.start()

    def spread(mine, board, others, send, recv):
        return [
            remote(board.at[mine], board.at[mine], send.at[d], recv.at[d], other)
            for d, other in enumerate(others)
        ]

    def drain(board, others, send, recv):
        for d, other in enumerate(others):
            copy = remote(board.at[0], board.at[0], send.at[d], recv.at[d], other)
            copy.wait_send()
            copy.wait_recv()

    cost_lon[lo] = jnp.full((8, 128), cost, jnp.float32)
    for copy in spread(lo, cost_lon, lon_others, lon_send, lon_recv):
        copy.start()

    for k in range(STEPS):
        final = k == STEPS - 1
        slot = STEPS + k
        step(slot, None if final else slot + 1, False, None if final else STEPS - 2 - k, not final)
        if k == 1:
            drain(cost_lon, lon_others, lon_send, lon_recv)
            cost_lat[la] = jnp.sum(cost_lon[...], axis=0)
            for copy in spread(la, cost_lat, lat_others, lat_send, lat_recv):
                copy.start()
    drain(cost_lat, lat_others, lat_send, lat_recv)
    cost_ref[...] = jnp.sum(cost_lat[...], axis=0)

    for copy in face_copies:
        copy.wait_send()
    for t in range(2 * STEPS):
        for copy in row_copies(t) + col_copies(t):
            copy.wait_send()


def on_device(
    n_lat, n_lon,
    initial, east_wind, north_wind, east_mask, north_mask, mixing,
    obs_cell, obs_level, obs_value, obs_weight,
):
    levels, rows, cols = initial.shape
    n_obs = obs_cell.shape[-1]
    flat = (levels * rows, cols)
    f32 = jnp.float32
    vmem = pl.BlockSpec(memory_space=pltpu.VMEM)
    dma = pltpu.SemaphoreType.DMA
    gradient, cost = pl.pallas_call(
        functools.partial(window, n_lat, n_lon, levels, rows, cols),
        out_shape=(jax.ShapeDtypeStruct(flat, f32), jax.ShapeDtypeStruct((8, 128), f32)),
        in_specs=[vmem] * 5 + [pl.BlockSpec(memory_space=pltpu.SMEM)] + [vmem] * 4,
        out_specs=(vmem, vmem),
        scratch_shapes=[
            pltpu.VMEM((2 * STEPS + 1, rows, levels, cols), f32),
            pltpu.VMEM((STEPS - 1,) + flat, f32),
            pltpu.VMEM((rows, levels, cols), f32),
            pltpu.VMEM((rows, levels, cols), f32),
            pltpu.VMEM((rows, levels, cols), f32),
            pltpu.VMEM((rows, levels, cols), f32),
            pltpu.VMEM((rows, levels, cols), f32),
            pltpu.VMEM((rows + 1, levels, cols), f32),
            pltpu.VMEM((rows + 1, levels, cols), f32),
            pltpu.VMEM((levels, cols), f32),
            pltpu.VMEM((levels, cols), f32),
            pltpu.VMEM((2 * STEPS, 2, levels, cols), f32),
            pltpu.VMEM((2 * STEPS, 2, levels, cols), f32),
            pltpu.VMEM((2 * STEPS, levels, cols), f32),
            pltpu.VMEM((levels, cols), f32),
            pltpu.VMEM((levels, cols), f32),
            pltpu.VMEM((n_lon, 8, 128), f32),
            pltpu.VMEM((n_lat, 8, 128), f32),
            dma((2 * STEPS, 4)),
            dma((2 * STEPS, 4)),
            dma((3,)),
            dma((3,)),
            dma((n_lon - 1,)),
            dma((n_lon - 1,)),
            dma((n_lat - 1,)),
            dma((n_lat - 1,)),
        ],
        compiler_params=pltpu.CompilerParams(
            collective_id=0, has_side_effects=True, vmem_limit_bytes=48 * 1024 * 1024
        ),
        cost_estimate=pl.CostEstimate(
            flops=8 * 14 * levels * rows * cols, bytes_accessed=24 * levels * rows * cols, transcendentals=0
        ),
    )(
        initial.reshape(flat), east_wind.reshape(flat), north_wind.reshape(flat),
        east_mask.reshape(flat), north_mask.reshape(flat), mixing,
        obs_cell.reshape(STEPS, n_obs), obs_level.reshape(STEPS, n_obs),
        obs_value.reshape(STEPS, n_obs), obs_weight.reshape(STEPS, n_obs),
    )
    return gradient.reshape(levels, rows, cols), cost[0, 0]


def solution(mesh):
    grid = P(None, "lat", "lon")
    spots = P("lat", "lon", None, None)
    return jax.shard_map(
        functools.partial(on_device, mesh.shape["lat"], mesh.shape["lon"]),
        mesh=mesh,
        in_specs=(grid,) * 5 + (P(),) + (spots,) * 4,
        out_specs=(grid, P()),
        check_vma=False,
    )
```

```python
import functools

import jax
import jax.numpy as jnp
from jax import lax
from jax.experimental import pallas as pl
from jax.experimental.pallas import tpu as pltpu
from jax.sharding import PartitionSpec as P

STEPS = 4
MESH = pl.DeviceIdType.MESH


def halves(value):
    top = value.astype(jnp.bfloat16)
    return top, (value - top.astype(jnp.float32)).astype(jnp.bfloat16)


def window(
    n_lat, n_lon, levels, rows, cols,
    *refs,
):
    sources, (grad_ref, cost_ref), landed, rest = refs[:10], refs[10:12], refs[12:22], refs[22:]
    start_ref, ew_ref, nw_ref, em_ref, nm_ref, mix_ref = landed[:6]
    cell_ref, level_ref, value_ref, weight_ref = landed[6:]
    (
        field, source, diag, west_p, west_q, east_p, east_q, south_p, south_q,
        up, down, edge_row, edge_col, packed, face_out, face_in, cost_lon, cost_lat,
        send_sem, recv_sem, face_send, face_recv, lon_send, lon_recv, lat_send, lat_recv, load_sem,
    ) = rest
    la, lo = lax.axis_index("lat"), lax.axis_index("lon")
    north = (lax.rem(la + 1, n_lat), lo)
    south = (lax.rem(la + n_lat - 1, n_lat), lo)
    east = (la, lax.rem(lo + 1, n_lon))
    west = (la, lax.rem(lo + n_lon - 1, n_lon))
    lat_others = [(lax.rem(la + d, n_lat), lo) for d in range(1, n_lat)]
    lon_others = [(la, lax.rem(lo + d, n_lon)) for d in range(1, n_lon)]

    loads = [
        pltpu.make_async_copy(src, dst, load_sem.at[i])
        for i, (src, dst) in enumerate(zip(sources, landed))
    ]
    for load in loads:
        load.start()
    barrier = pltpu.get_barrier_semaphore()
    for other in lat_others + lon_others:
        pl.semaphore_signal(barrier, inc=1, device_id=other, device_id_type=MESH)

    lane = lax.broadcasted_iota(jnp.int32, (levels, cols), 1)
    first, last = lane == 0, lane == cols - 1

    def remote(src, dst, send, recv, target):
        return pltpu.make_async_remote_copy(
            src_ref=src, dst_ref=dst, send_sem=send, recv_sem=recv,
            device_id=target, device_id_type=MESH,
        )

    def row_copies(t):
        return (
            remote(field.at[t, 0], edge_row.at[t, 1], send_sem.at[t, 0], recv_sem.at[t, 0], south),
            remote(field.at[t, rows - 1], edge_row.at[t, 0], send_sem.at[t, 1], recv_sem.at[t, 1], north),
        )

    def col_copies(t):
        return (
            remote(packed.at[t], edge_col.at[t, 1], send_sem.at[t, 2], recv_sem.at[t, 2], west),
            remote(packed.at[t], edge_col.at[t, 0], send_sem.at[t, 3], recv_sem.at[t, 3], east),
        )

    face_copies = (
        remote(face_out, face_in, face_send.at[0], face_recv.at[0], west),
        remote(south_p.at[0], south_p.at[rows], face_send.at[1], face_recv.at[1], south),
        remote(south_q.at[0], south_q.at[rows], face_send.at[2], face_recv.at[2], south),
    )

    def pack(total, value, row):
        turned = pltpu.roll(value, 2 * row, 1)
        spot = (lane == 2 * row) | (lane == (2 * row + cols - 1) % cols)
        return jnp.where(spot, turned, total)

    def strided(ref, row):
        return ref[pl.ds(row, levels, stride=rows), :]

    def parts(wind, mask):
        share = jnp.where(mask == 1, jnp.where(wind > 0, 1.0, 0.0), 0.5)
        return wind * share, wind * (1.0 - share)

    for load in loads[:5]:
        load.wait()
    edges = jnp.zeros((levels, cols), jnp.float32)
    faces = jnp.zeros((levels, cols), jnp.float32)
    for row in range(rows):
        value = strided(start_ref, row)
        field[0, row] = value
        edges = pack(edges, value, row)
        p, q = parts(strided(ew_ref, row), strided(em_ref, row))
        west_p[row] = p
        west_q[row] = -q
        faces = jnp.where(lane == 2 * row, pltpu.roll(p, 2 * row, 1), faces)
        faces = jnp.where(lane == 2 * row + 1, pltpu.roll(q, 2 * row + 1, 1), faces)
        p, q = parts(strided(nw_ref, row), strided(nm_ref, row))
        if row == 0:
            p = jnp.where(la > 0, p, 0.0)
            q = jnp.where(la > 0, q, 0.0)
        south_p[row] = p
        south_q[row] = -q
    packed[0] = edges
    face_out[...] = faces

    pl.semaphore_wait(barrier, n_lat + n_lon - 2)
    for copy in face_copies + row_copies(0) + col_copies(0):
        copy.start()

    for load in loads[5:]:
        load.wait()
    up[levels - 1 : levels, :] = jnp.zeros((1, cols), jnp.float32)
    down[0:1, :] = jnp.zeros((1, cols), jnp.float32)
    for level in range(levels - 1):
        line = jnp.full((1, cols), mix_ref[level], jnp.float32)
        up[level : level + 1, :] = line
        down[level + 1 : level + 2, :] = line

    for copy in face_copies:
        copy.wait_recv()
    column = 1.0 - up[...] - down[...]
    got = face_in[...]
    for row in range(rows):
        p, q = west_p[row], west_q[row]
        turned_p = pltpu.roll(got, (cols - 2 * row) % cols, 1)
        turned_q = -pltpu.roll(got, (cols - 2 * row - 1) % cols, 1)
        p_next = pltpu.roll(jnp.where(first, turned_p, p), cols - 1, 1)
        q_next = pltpu.roll(jnp.where(first, turned_q, q), cols - 1, 1)
        east_p[row] = p_next
        east_q[row] = q_next
        diag[row] = column - q - p_next - south_q[row] - south_p[row + 1]

    def step(t, out, forward, extra, send):
        for copy in row_copies(t) + col_copies(t):
            copy.wait_recv()
        cw, ce, cs, cn = (
            (west_p, east_q, south_p, south_q) if forward else (west_q, east_p, south_q, south_p)
        )
        edge = jnp.where(lax.rem(lane, 2) == 0, edge_col[t, 1], edge_col[t, 0])

        def one(row, below, above):
            value = field[t, row]
            turned = pltpu.roll(edge, (cols - 2 * row) % cols, 1)
            at_west = pltpu.roll(jnp.where(last, turned, value), 1, 1)
            at_east = pltpu.roll(jnp.where(first, turned, value), cols - 1, 1)
            higher = pltpu.roll(value, levels - 1, 0)
            lower = pltpu.roll(value, 1, 0)
            new = (
                (diag[row] * value + cw[row] * at_west)
                + (ce[row] * at_east + cs[row] * below)
                + (cn[row + 1] * above + up[...] * higher)
                + down[...] * lower
            )
            if extra is not None:
                new = new + source[extra, row * levels : (row + 1) * levels, :]
            return new

        def put(row, new):
            if out is None:
                grad_ref[pl.ds(row, levels, stride=rows), :] = new
            else:
                field[out, row] = new

        low = one(0, edge_row[t, 0], field[t, 1])
        put(0, low)
        high = one(rows - 1, field[t, rows - 2], edge_row[t, 1])
        put(rows - 1, high)
        if send:
            for copy in row_copies(out):
                copy.start()
        total = pack(pack(jnp.zeros_like(low), low, 0), high, rows - 1)

        for row in range(1, rows - 1):
            new = one(row, field[t, row - 1], field[t, row + 1])
            put(row, new)
            if send:
                total = pack(total, new, row)
        if send:
            packed[out] = total
            for copy in col_copies(out):
                copy.start()

    def observe(k, slot):
        n_obs = cell_ref.shape[1]
        cell = cell_ref[k : k + 1, :]
        place = (cell // cols) * levels + level_ref[k : k + 1, :]
        col = lax.rem(cell, cols)
        cols_hot = lax.broadcasted_iota(jnp.int32, (cols, n_obs), 0) == col
        pick = jnp.where(cols_hot, 1.0, 0.0).astype(jnp.bfloat16)
        pick = jnp.concatenate([pick, pick], 0)
        group = 4 * levels
        spots = lax.broadcasted_iota(jnp.int32, (group, n_obs), 0)

        found = jnp.zeros((8, n_obs), jnp.float32)
        for row in range(0, rows, 4):
            value = field[slot, row : row + 4].reshape(group, cols)
            values = jnp.dot(
                jnp.concatenate(halves(value), 1), pick, preferred_element_type=jnp.float32
            )
            values = jnp.where(spots == place - row * levels, values, 0.0)
            found = found + jnp.sum(values.reshape(group // 8, 8, n_obs), axis=0)
        innovation = jnp.sum(found, axis=0, keepdims=True) - value_ref[k : k + 1, :]
        weighted = weight_ref[k : k + 1, :] * innovation
        share = jnp.concatenate(halves(jnp.where(cols_hot, weighted, 0.0)), 0)

        for row in range(0, rows, 4):
            hot = jnp.where(spots == place - row * levels, 1.0, 0.0).astype(jnp.bfloat16)
            both = lax.dot_general(
                hot, share, (((1,), (1,)), ((), ())), preferred_element_type=jnp.float32
            )
            value = both[:, :cols] + both[:, cols:]
            if k == STEPS - 1:
                field[STEPS, row : row + 4] = value.reshape(4, levels, cols)
            else:
                source[k, row * levels : row * levels + group, :] = value
        return 0.5 * jnp.sum(weighted * innovation)

    cost = jnp.zeros((), jnp.float32)
    for k in range(STEPS):
        final = k == STEPS - 1
        slot = 2 * STEPS if final else k + 1
        step(k, slot, True, None, not final)
        cost = cost + observe(k, slot)

    for copy in row_copies(STEPS):
        copy.start()
    total = jnp.zeros((levels, cols), jnp.float32)
    for row in range(rows):
        total = pack(total, field[STEPS, row], row)
    packed[STEPS] = total
    for copy in col_copies(STEPS):
        copy.start()

    def spread(mine, board, others, send, recv):
        return [
            remote(board.at[mine], board.at[mine], send.at[d], recv.at[d], other)
            for d, other in enumerate(others)
        ]

    def drain(board, others, send, recv):
        for d, other in enumerate(others):
            copy = remote(board.at[0], board.at[0], send.at[d], recv.at[d], other)
            copy.wait_send()
            copy.wait_recv()

    cost_lon[lo] = jnp.full((8, 128), cost, jnp.float32)
    for copy in spread(lo, cost_lon, lon_others, lon_send, lon_recv):
        copy.start()

    for k in range(STEPS):
        final = k == STEPS - 1
        slot = STEPS + k
        step(slot, None if final else slot + 1, False, None if final else STEPS - 2 - k, not final)
        if k == 1:
            drain(cost_lon, lon_others, lon_send, lon_recv)
            cost_lat[la] = jnp.sum(cost_lon[...], axis=0)
            for copy in spread(la, cost_lat, lat_others, lat_send, lat_recv):
                copy.start()
    drain(cost_lat, lat_others, lat_send, lat_recv)
    cost_ref[0, 0] = jnp.sum(cost_lat[...], axis=0)[0, 0]

    for copy in face_copies:
        copy.wait_send()
    for t in range(2 * STEPS):
        for copy in row_copies(t) + col_copies(t):
            copy.wait_send()


def on_device(
    n_lat, n_lon,
    initial, east_wind, north_wind, east_mask, north_mask, mixing,
    obs_cell, obs_level, obs_value, obs_weight,
):
    levels, rows, cols = initial.shape
    n_obs = obs_cell.shape[-1]
    flat = (levels * rows, cols)
    f32 = jnp.float32
    vmem = pl.BlockSpec(memory_space=pltpu.VMEM)
    dma = pltpu.SemaphoreType.DMA
    gradient, cost = pl.pallas_call(
        functools.partial(window, n_lat, n_lon, levels, rows, cols),
        out_shape=(jax.ShapeDtypeStruct(flat, f32), jax.ShapeDtypeStruct((1, 1), f32)),
        in_specs=[pl.BlockSpec(memory_space=pl.ANY)] * 10,
        out_specs=(vmem, pl.BlockSpec(memory_space=pltpu.SMEM)),
        scratch_shapes=[
            pltpu.VMEM(flat, f32),
            pltpu.VMEM(flat, f32),
            pltpu.VMEM(flat, f32),
            pltpu.VMEM(flat, jnp.int32),
            pltpu.VMEM(flat, jnp.int32),
            pltpu.SMEM(mixing.shape, f32),
            pltpu.VMEM((STEPS, n_obs), jnp.int32),
            pltpu.VMEM((STEPS, n_obs), jnp.int32),
            pltpu.VMEM((STEPS, n_obs), f32),
            pltpu.VMEM((STEPS, n_obs), f32),
            pltpu.VMEM((2 * STEPS + 1, rows, levels, cols), f32),
            pltpu.VMEM((STEPS - 1,) + flat, f32),
            pltpu.VMEM((rows, levels, cols), f32),
            pltpu.VMEM((rows, levels, cols), f32),
            pltpu.VMEM((rows, levels, cols), f32),
            pltpu.VMEM((rows, levels, cols), f32),
            pltpu.VMEM((rows, levels, cols), f32),
            pltpu.VMEM((rows + 1, levels, cols), f32),
            pltpu.VMEM((rows + 1, levels, cols), f32),
            pltpu.VMEM((levels, cols), f32),
            pltpu.VMEM((levels, cols), f32),
            pltpu.VMEM((2 * STEPS, 2, levels, cols), f32),
            pltpu.VMEM((2 * STEPS, 2, levels, cols), f32),
            pltpu.VMEM((2 * STEPS, levels, cols), f32),
            pltpu.VMEM((levels, cols), f32),
            pltpu.VMEM((levels, cols), f32),
            pltpu.VMEM((n_lon, 8, 128), f32),
            pltpu.VMEM((n_lat, 8, 128), f32),
            dma((2 * STEPS, 4)),
            dma((2 * STEPS, 4)),
            dma((3,)),
            dma((3,)),
            dma((n_lon - 1,)),
            dma((n_lon - 1,)),
            dma((n_lat - 1,)),
            dma((n_lat - 1,)),
            dma((10,)),
        ],
        compiler_params=pltpu.CompilerParams(
            collective_id=0, has_side_effects=True, vmem_limit_bytes=48 * 1024 * 1024
        ),
        cost_estimate=pl.CostEstimate(
            flops=8 * 14 * levels * rows * cols, bytes_accessed=24 * levels * rows * cols, transcendentals=0
        ),
    )(
        initial.reshape(flat), east_wind.reshape(flat), north_wind.reshape(flat),
        east_mask.reshape(flat), north_mask.reshape(flat), mixing,
        obs_cell.reshape(STEPS, n_obs), obs_level.reshape(STEPS, n_obs),
        obs_value.reshape(STEPS, n_obs), obs_weight.reshape(STEPS, n_obs),
    )
    return gradient.reshape(levels, rows, cols), cost[0, 0]


def solution(mesh):
    grid = P(None, "lat", "lon")
    spots = P("lat", "lon", None, None)
    return jax.shard_map(
        functools.partial(on_device, mesh.shape["lat"], mesh.shape["lon"]),
        mesh=mesh,
        in_specs=(grid,) * 5 + (P(),) + (spots,) * 4,
        out_specs=(grid, P()),
        check_vma=False,
    )
```

```python
import functools

import jax
import jax.numpy as jnp
from jax import lax
from jax.experimental import pallas as pl
from jax.experimental.pallas import tpu as pltpu
from jax.sharding import PartitionSpec as P

STEPS = 4
MESH = pl.DeviceIdType.MESH


def halves(value):
    top = value.astype(jnp.bfloat16)
    return top, (value - top.astype(jnp.float32)).astype(jnp.bfloat16)


def window(
    n_lat, n_lon, levels, rows, cols,
    *refs,
):
    sources, (grad_ref, cost_ref), landed, rest = refs[:10], refs[10:12], refs[12:22], refs[22:]
    start_ref, ew_ref, nw_ref, em_ref, nm_ref, mix_ref = landed[:6]
    cell_ref, level_ref, value_ref, weight_ref = landed[6:]
    (
        field, source, diag, west_p, west_q, east_p, east_q, south_p, south_q,
        up, down, edge_row, edge_col, packed, face_out, face_in, cost_lon, cost_lat,
        send_sem, recv_sem, face_send, face_recv, lon_send, lon_recv, lat_send, lat_recv, load_sem,
    ) = rest
    la, lo = lax.axis_index("lat"), lax.axis_index("lon")
    north = (lax.rem(la + 1, n_lat), lo)
    south = (lax.rem(la + n_lat - 1, n_lat), lo)
    east = (la, lax.rem(lo + 1, n_lon))
    west = (la, lax.rem(lo + n_lon - 1, n_lon))
    lat_others = [(lax.rem(la + d, n_lat), lo) for d in range(1, n_lat)]
    lon_others = [(la, lax.rem(lo + d, n_lon)) for d in range(1, n_lon)]

    loads = [
        pltpu.make_async_copy(src, dst, load_sem.at[i])
        for i, (src, dst) in enumerate(zip(sources, landed))
    ]
    for load in loads:
        load.start()
    barrier = pltpu.get_barrier_semaphore()
    for other in lat_others + lon_others:
        pl.semaphore_signal(barrier, inc=1, device_id=other, device_id_type=MESH)

    groups = cols // (2 * rows)
    fold = levels // groups
    lane = lax.broadcasted_iota(jnp.int32, (levels, cols), 1)
    first, last = lane == 0, lane == cols - 1
    rim = first | last
    thin = lax.broadcasted_iota(jnp.int32, (fold, cols), 1)
    even = lax.rem(thin, 2) == 0

    def remote(src, dst, send, recv, target):
        return pltpu.make_async_remote_copy(
            src_ref=src, dst_ref=dst, send_sem=send, recv_sem=recv,
            device_id=target, device_id_type=MESH,
        )

    def row_copies(t):
        return (
            remote(field.at[t, 0], edge_row.at[t, 1], send_sem.at[t, 0], recv_sem.at[t, 0], south),
            remote(field.at[t, rows - 1], edge_row.at[t, 0], send_sem.at[t, 1], recv_sem.at[t, 1], north),
        )

    def col_copies(t):
        return (
            remote(packed.at[t], edge_col.at[t, 1], send_sem.at[t, 2], recv_sem.at[t, 2], west),
            remote(packed.at[t], edge_col.at[t, 0], send_sem.at[t, 3], recv_sem.at[t, 3], east),
        )

    face_copies = (
        remote(face_out, face_in, face_send.at[0], face_recv.at[0], west),
        remote(south_p.at[0], south_p.at[rows], face_send.at[1], face_recv.at[1], south),
        remote(south_q.at[0], south_q.at[rows], face_send.at[2], face_recv.at[2], south),
    )

    def pack(total, value, row):
        for group in range(groups):
            shift = 2 * row + 2 * rows * group
            turned = pltpu.roll(value[group * fold : (group + 1) * fold], shift, 1)
            spot = (thin == shift) | (thin == (shift + cols - 1) % cols)
            total = jnp.where(spot, turned, total)
        return total

    def unpack(total, row, more=0):
        return jnp.concatenate(
            [
                pltpu.roll(total, (2 * cols - 2 * row - 2 * rows * group - more) % cols, 1)
                for group in range(groups)
            ],
            0,
        )

    def strided(ref, row):
        return ref[pl.ds(row, levels, stride=rows), :]

    def parts(wind, mask):
        share = jnp.where(mask == 1, jnp.where(wind > 0, 1.0, 0.0), 0.5)
        return wind * share, wind * (1.0 - share)

    loads[0].wait()
    edges = jnp.zeros((fold, cols), jnp.float32)
    for row in range(rows):
        value = strided(start_ref, row)
        field[0, row] = value
        edges = pack(edges, value, row)
    packed[0] = edges
    pl.semaphore_wait(barrier, n_lat + n_lon - 2)
    for copy in row_copies(0) + col_copies(0):
        copy.start()

    for load in loads[1:5]:
        load.wait()
    faces = jnp.zeros((fold, cols), jnp.float32)
    for row in range(rows):
        p, q = parts(strided(nw_ref, row), strided(nm_ref, row))
        if row == 0:
            p = jnp.where(la > 0, p, 0.0)
            q = jnp.where(la > 0, q, 0.0)
        south_p[row] = p
        south_q[row] = -q
        own = 1.0 + q
        p, q = parts(strided(ew_ref, row), strided(em_ref, row))
        west_p[row] = jnp.where(first, 0.0, p)
        west_q[row] = jnp.where(first, 0.0, -q)
        p_next = jnp.where(last, 0.0, pltpu.roll(p, cols - 1, 1))
        east_p[row] = p_next
        east_q[row] = jnp.where(last, 0.0, -pltpu.roll(q, cols - 1, 1))
        diag[row] = own + q - p_next
        for group in range(groups):
            shift = 2 * row + 2 * rows * group
            part = slice(group * fold, (group + 1) * fold)
            faces = jnp.where(thin == shift, pltpu.roll(p[part], shift, 1), faces)
            faces = jnp.where(thin == shift + 1, pltpu.roll(q[part], shift + 1, 1), faces)
    face_out[...] = faces
    for copy in face_copies:
        copy.start()

    for load in loads[5:]:
        load.wait()
    up[levels - 1 : levels, :] = jnp.zeros((1, cols), jnp.float32)
    down[0:1, :] = jnp.zeros((1, cols), jnp.float32)
    for level in range(levels - 1):
        line = jnp.full((1, cols), mix_ref[level], jnp.float32)
        up[level : level + 1, :] = line
        down[level + 1 : level + 2, :] = line

    for copy in face_copies:
        copy.wait_recv()
    column = up[...] + down[...]
    got = face_in[...]
    for row in range(rows):
        p_next = jnp.where(last, unpack(got, row, 1), 0.0)
        diag[row] = diag[row] - column - p_next - south_p[row + 1]
    rim_ahead = jnp.where(even, faces, -pltpu.roll(got, cols - 2, 1))
    rim_back = jnp.where(even, -pltpu.roll(faces, cols - 1, 1), pltpu.roll(got, cols - 1, 1))

    def coefs(forward):
        if forward:
            return west_p, east_q, south_p, south_q
        return west_q, east_p, south_q, south_p

    def put(out, row, new):
        if out is None:
            grad_ref[pl.ds(row, levels, stride=rows), :] = new
        else:
            field[out, row] = new

    def get(out, row):
        if out is None:
            return grad_ref[pl.ds(row, levels, stride=rows), :]
        return field[out, row]

    def inside(t, out, forward, extra, send):
        cw, ce, cs, cn = coefs(forward)
        total = jnp.zeros((fold, cols), jnp.float32)
        for row in range(rows):
            value = field[t, row]
            new = (
                (diag[row] * value + cw[row] * pltpu.roll(value, 1, 1))
                + (ce[row] * pltpu.roll(value, cols - 1, 1) + up[...] * pltpu.roll(value, levels - 1, 0))
                + down[...] * pltpu.roll(value, 1, 0)
            )
            if row > 0:
                new = new + cs[row] * field[t, row - 1]
            if row < rows - 1:
                new = new + cn[row + 1] * field[t, row + 1]
            if extra is not None:
                new = new + source[extra, row * levels : (row + 1) * levels, :]
            put(out, row, new)
            if send and 0 < row < rows - 1:
                total = pack(total, new, row)
        return total

    def finish(t, out, forward, total, send):
        cw, ce, cs, cn = coefs(forward)
        for copy in row_copies(t) + col_copies(t):
            copy.wait_recv()
        met = jnp.where(
            even, pltpu.roll(edge_col[t, 0], 1, 1), pltpu.roll(edge_col[t, 1], cols - 1, 1)
        )
        gain = (rim_ahead if forward else rim_back) * met
        low = get(out, 0) + cs[0] * edge_row[t, 0]
        high = get(out, rows - 1) + cn[rows] * edge_row[t, 1]
        put(out, 0, low + jnp.where(rim, unpack(gain, 0), 0.0))
        put(out, rows - 1, high + jnp.where(rim, unpack(gain, rows - 1), 0.0))
        if send:
            packed[out] = pack(pack(total, low, 0), high, rows - 1) + gain
            for copy in col_copies(out) + row_copies(out):
                copy.start()
        for row in range(1, rows - 1):
            put(out, row, get(out, row) + jnp.where(rim, unpack(gain, row), 0.0))

    def observe(k, slot):
        n_obs = cell_ref.shape[1]
        cell = cell_ref[k : k + 1, :]
        place = (cell // cols) * levels + level_ref[k : k + 1, :]
        col = lax.rem(cell, cols)
        cols_hot = lax.broadcasted_iota(jnp.int32, (cols, n_obs), 0) == col
        pick = jnp.where(cols_hot, 1.0, 0.0).astype(jnp.bfloat16)
        pick = jnp.concatenate([pick, pick], 0)
        group = 4 * levels
        spots = lax.broadcasted_iota(jnp.int32, (group, n_obs), 0)

        found = jnp.zeros((8, n_obs), jnp.float32)
        for row in range(0, rows, 4):
            value = field[slot, row : row + 4].reshape(group, cols)
            values = jnp.dot(
                jnp.concatenate(halves(value), 1), pick, preferred_element_type=jnp.float32
            )
            values = jnp.where(spots == place - row * levels, values, 0.0)
            found = found + jnp.sum(values.reshape(group // 8, 8, n_obs), axis=0)
        innovation = jnp.sum(found, axis=0, keepdims=True) - value_ref[k : k + 1, :]
        weighted = weight_ref[k : k + 1, :] * innovation
        share = jnp.concatenate(halves(jnp.where(cols_hot, weighted, 0.0)), 0)

        for row in range(0, rows, 4):
            hot = jnp.where(spots == place - row * levels, 1.0, 0.0).astype(jnp.bfloat16)
            both = lax.dot_general(
                hot, share, (((1,), (1,)), ((), ())), preferred_element_type=jnp.float32
            )
            value = both[:, :cols] + both[:, cols:]
            if k == STEPS - 1:
                field[STEPS, row : row + 4] = value.reshape(4, levels, cols)
            else:
                source[k, row * levels : row * levels + group, :] = value
        return 0.5 * jnp.sum(weighted * innovation)

    cost = jnp.zeros((), jnp.float32)
    total = inside(0, 1, True, None, True)
    for k in range(STEPS):
        final = k == STEPS - 1
        slot = 2 * STEPS if final else k + 1
        finish(k, slot, True, total, not final)
        if not final:
            ahead = k + 1 == STEPS - 1
            total = inside(k + 1, 2 * STEPS if ahead else k + 2, True, None, not ahead)
        cost = cost + observe(k, slot)

    for copy in row_copies(STEPS):
        copy.start()
    total = jnp.zeros((fold, cols), jnp.float32)
    for row in range(rows):
        total = pack(total, field[STEPS, row], row)
    packed[STEPS] = total
    for copy in col_copies(STEPS):
        copy.start()

    def spread(mine, board, others, send, recv):
        return [
            remote(board.at[mine], board.at[mine], send.at[d], recv.at[d], other)
            for d, other in enumerate(others)
        ]

    def drain(board, others, send, recv):
        for d, other in enumerate(others):
            copy = remote(board.at[0], board.at[0], send.at[d], recv.at[d], other)
            copy.wait_send()
            copy.wait_recv()

    cost_lon[lo] = jnp.full((8, 128), cost, jnp.float32)
    for copy in spread(lo, cost_lon, lon_others, lon_send, lon_recv):
        copy.start()

    for k in range(STEPS):
        final = k == STEPS - 1
        slot = STEPS + k
        out = None if final else slot + 1
        total = inside(slot, out, False, None if final else STEPS - 2 - k, not final)
        finish(slot, out, False, total, not final)
        if k == 1:
            drain(cost_lon, lon_others, lon_send, lon_recv)
            cost_lat[la] = jnp.sum(cost_lon[...], axis=0)
            for copy in spread(la, cost_lat, lat_others, lat_send, lat_recv):
                copy.start()
    drain(cost_lat, lat_others, lat_send, lat_recv)
    cost_ref[0, 0] = jnp.sum(cost_lat[...], axis=0)[0, 0]

    for copy in face_copies:
        copy.wait_send()
    for t in range(2 * STEPS):
        for copy in row_copies(t) + col_copies(t):
            copy.wait_send()


def on_device(
    n_lat, n_lon,
    initial, east_wind, north_wind, east_mask, north_mask, mixing,
    obs_cell, obs_level, obs_value, obs_weight,
):
    levels, rows, cols = initial.shape
    n_obs = obs_cell.shape[-1]
    flat = (levels * rows, cols)
    f32 = jnp.float32
    fold = levels * 2 * rows // cols
    vmem = pl.BlockSpec(memory_space=pltpu.VMEM)
    dma = pltpu.SemaphoreType.DMA
    gradient, cost = pl.pallas_call(
        functools.partial(window, n_lat, n_lon, levels, rows, cols),
        out_shape=(jax.ShapeDtypeStruct(flat, f32), jax.ShapeDtypeStruct((1, 1), f32)),
        in_specs=[pl.BlockSpec(memory_space=pl.ANY)] * 10,
        out_specs=(vmem, pl.BlockSpec(memory_space=pltpu.SMEM)),
        scratch_shapes=[
            pltpu.VMEM(flat, f32),
            pltpu.VMEM(flat, f32),
            pltpu.VMEM(flat, f32),
            pltpu.VMEM(flat, jnp.int32),
            pltpu.VMEM(flat, jnp.int32),
            pltpu.SMEM(mixing.shape, f32),
            pltpu.VMEM((STEPS, n_obs), jnp.int32),
            pltpu.VMEM((STEPS, n_obs), jnp.int32),
            pltpu.VMEM((STEPS, n_obs), f32),
            pltpu.VMEM((STEPS, n_obs), f32),
            pltpu.VMEM((2 * STEPS + 1, rows, levels, cols), f32),
            pltpu.VMEM((STEPS - 1,) + flat, f32),
            pltpu.VMEM((rows, levels, cols), f32),
            pltpu.VMEM((rows, levels, cols), f32),
            pltpu.VMEM((rows, levels, cols), f32),
            pltpu.VMEM((rows, levels, cols), f32),
            pltpu.VMEM((rows, levels, cols), f32),
            pltpu.VMEM((rows + 1, levels, cols), f32),
            pltpu.VMEM((rows + 1, levels, cols), f32),
            pltpu.VMEM((levels, cols), f32),
            pltpu.VMEM((levels, cols), f32),
            pltpu.VMEM((2 * STEPS, 2, levels, cols), f32),
            pltpu.VMEM((2 * STEPS, 2, fold, cols), f32),
            pltpu.VMEM((2 * STEPS, fold, cols), f32),
            pltpu.VMEM((fold, cols), f32),
            pltpu.VMEM((fold, cols), f32),
            pltpu.VMEM((n_lon, 8, 128), f32),
            pltpu.VMEM((n_lat, 8, 128), f32),
            dma((2 * STEPS, 4)),
            dma((2 * STEPS, 4)),
            dma((3,)),
            dma((3,)),
            dma((n_lon - 1,)),
            dma((n_lon - 1,)),
            dma((n_lat - 1,)),
            dma((n_lat - 1,)),
            dma((10,)),
        ],
        compiler_params=pltpu.CompilerParams(
            collective_id=0, has_side_effects=True, vmem_limit_bytes=62 * 1024 * 1024
        ),
        cost_estimate=pl.CostEstimate(
            flops=8 * 14 * levels * rows * cols, bytes_accessed=24 * levels * rows * cols, transcendentals=0
        ),
    )(
        initial.reshape(flat), east_wind.reshape(flat), north_wind.reshape(flat),
        east_mask.reshape(flat), north_mask.reshape(flat), mixing,
        obs_cell.reshape(STEPS, n_obs), obs_level.reshape(STEPS, n_obs),
        obs_value.reshape(STEPS, n_obs), obs_weight.reshape(STEPS, n_obs),
    )
    return gradient.reshape(levels, rows, cols), cost[0, 0]


def solution(mesh):
    grid = P(None, "lat", "lon")
    spots = P("lat", "lon", None, None)
    return jax.shard_map(
        functools.partial(on_device, mesh.shape["lat"], mesh.shape["lon"]),
        mesh=mesh,
        in_specs=(grid,) * 5 + (P(),) + (spots,) * 4,
        out_specs=(grid, P()),
        check_vma=False,
    )
```

```python
import functools

import jax
import jax.numpy as jnp
from jax import lax
from jax.experimental import pallas as pl
from jax.experimental.pallas import tpu as pltpu
from jax.sharding import PartitionSpec as P

STEPS = 4
MESH = pl.DeviceIdType.MESH


def halves(value):
    top = value.astype(jnp.bfloat16)
    return top, (value - top.astype(jnp.float32)).astype(jnp.bfloat16)


def window(
    n_lat, n_lon, levels, rows, cols,
    *refs,
):
    sources, (grad_ref, cost_ref), landed, rest = refs[:10], refs[10:12], refs[12:22], refs[22:]
    start_ref, ew_ref, nw_ref, em_ref, nm_ref, mix_ref = landed[:6]
    cell_ref, level_ref, value_ref, weight_ref = landed[6:]
    (
        field, source, diag, west_p, west_q, east_p, east_q, south_p, south_q,
        up, down, edge_row, edge_col, packed, face_out, face_in, cost_lon, cost_lat,
        send_sem, recv_sem, face_send, face_recv, lon_send, lon_recv, lat_send, lat_recv, load_sem,
    ) = rest
    la, lo = lax.axis_index("lat"), lax.axis_index("lon")
    north = (lax.rem(la + 1, n_lat), lo)
    south = (lax.rem(la + n_lat - 1, n_lat), lo)
    east = (la, lax.rem(lo + 1, n_lon))
    west = (la, lax.rem(lo + n_lon - 1, n_lon))
    lat_others = [(lax.rem(la + d, n_lat), lo) for d in range(1, n_lat)]
    lon_others = [(la, lax.rem(lo + d, n_lon)) for d in range(1, n_lon)]

    loads = [
        pltpu.make_async_copy(src, dst, load_sem.at[i])
        for i, (src, dst) in enumerate(zip(sources, landed))
    ]
    for load in loads:
        load.start()
    barrier = pltpu.get_barrier_semaphore()
    for other in lat_others + lon_others:
        pl.semaphore_signal(barrier, inc=1, device_id=other, device_id_type=MESH)

    groups = cols // (2 * rows)
    fold = levels // groups
    lane = lax.broadcasted_iota(jnp.int32, (levels, cols), 1)
    first, last = lane == 0, lane == cols - 1
    rim = first | last
    thin = lax.broadcasted_iota(jnp.int32, (fold, cols), 1)
    even = lax.rem(thin, 2) == 0

    def remote(src, dst, send, recv, target):
        return pltpu.make_async_remote_copy(
            src_ref=src, dst_ref=dst, send_sem=send, recv_sem=recv,
            device_id=target, device_id_type=MESH,
        )

    def row_copies(t):
        return (
            remote(field.at[t, 0], edge_row.at[t, 1], send_sem.at[t, 0], recv_sem.at[t, 0], south),
            remote(field.at[t, rows - 1], edge_row.at[t, 0], send_sem.at[t, 1], recv_sem.at[t, 1], north),
        )

    def col_copies(t):
        return (
            remote(packed.at[t], edge_col.at[t, 1], send_sem.at[t, 2], recv_sem.at[t, 2], west),
            remote(packed.at[t], edge_col.at[t, 0], send_sem.at[t, 3], recv_sem.at[t, 3], east),
        )

    face_copies = (
        remote(face_out, face_in, face_send.at[0], face_recv.at[0], west),
        remote(south_p.at[0], south_p.at[rows], face_send.at[1], face_recv.at[1], south),
        remote(south_q.at[0], south_q.at[rows], face_send.at[2], face_recv.at[2], south),
    )

    def pack(total, value, row):
        for group in range(groups):
            shift = 2 * row + 2 * rows * group
            turned = pltpu.roll(value[group * fold : (group + 1) * fold], shift, 1)
            spot = (thin == shift) | (thin == (shift + cols - 1) % cols)
            total = jnp.where(spot, turned, total)
        return total

    def unpack(total, row, more=0):
        return jnp.concatenate(
            [
                pltpu.roll(total, (2 * cols - 2 * row - 2 * rows * group - more) % cols, 1)
                for group in range(groups)
            ],
            0,
        )

    def strided(ref, row):
        return ref[pl.ds(row, levels, stride=rows), :]

    def parts(wind, mask):
        share = jnp.where(mask == 1, jnp.where(wind > 0, 1.0, 0.0), 0.5)
        return wind * share, wind * (1.0 - share)

    loads[0].wait()
    edges = jnp.zeros((fold, cols), jnp.float32)
    for row in range(rows):
        value = strided(start_ref, row)
        field[0, row] = value
        edges = pack(edges, value, row)
    packed[0] = edges
    pl.semaphore_wait(barrier, n_lat + n_lon - 2)
    for copy in row_copies(0) + col_copies(0):
        copy.start()

    for load in loads[1:5]:
        load.wait()
    faces = jnp.zeros((fold, cols), jnp.float32)
    for row in range(rows):
        p, q = parts(strided(nw_ref, row), strided(nm_ref, row))
        if row == 0:
            p = jnp.where(la > 0, p, 0.0)
            q = jnp.where(la > 0, q, 0.0)
        south_p[row] = p
        south_q[row] = -q
        own = 1.0 + q
        p, q = parts(strided(ew_ref, row), strided(em_ref, row))
        west_p[row] = jnp.where(first, 0.0, p)
        west_q[row] = jnp.where(first, 0.0, -q)
        p_next = jnp.where(last, 0.0, pltpu.roll(p, cols - 1, 1))
        east_p[row] = p_next
        east_q[row] = jnp.where(last, 0.0, -pltpu.roll(q, cols - 1, 1))
        diag[row] = own + q - p_next
        for group in range(groups):
            shift = 2 * row + 2 * rows * group
            part = slice(group * fold, (group + 1) * fold)
            faces = jnp.where(thin == shift, pltpu.roll(p[part], shift, 1), faces)
            faces = jnp.where(thin == shift + 1, pltpu.roll(q[part], shift + 1, 1), faces)
    face_out[...] = faces
    for copy in face_copies:
        copy.start()

    for load in loads[5:]:
        load.wait()
    up[levels - 1 : levels, :] = jnp.zeros((1, cols), jnp.float32)
    down[0:1, :] = jnp.zeros((1, cols), jnp.float32)
    for level in range(levels - 1):
        line = jnp.full((1, cols), mix_ref[level], jnp.float32)
        up[level : level + 1, :] = line
        down[level + 1 : level + 2, :] = line

    for copy in face_copies:
        copy.wait_recv()
    column = up[...] + down[...]
    got = face_in[...]
    for row in range(rows):
        p_next = jnp.where(last, unpack(got, row, 1), 0.0)
        diag[row] = diag[row] - column - p_next - south_p[row + 1]
    rim_ahead = jnp.where(even, faces, -pltpu.roll(got, cols - 2, 1))
    rim_back = jnp.where(even, -pltpu.roll(faces, cols - 1, 1), pltpu.roll(got, cols - 1, 1))

    def coefs(forward):
        if forward:
            return west_p, east_q, south_p, south_q
        return west_q, east_p, south_q, south_p

    def put(out, row, new):
        if out is None:
            grad_ref[pl.ds(row, levels, stride=rows), :] = new
        else:
            field[out, row] = new

    def get(out, row):
        if out is None:
            return grad_ref[pl.ds(row, levels, stride=rows), :]
        return field[out, row]

    def inside(t, out, forward, extra):
        cw, ce, cs, cn = coefs(forward)
        total = jnp.zeros((fold, cols), jnp.float32)
        for row in range(rows):
            value = field[t, row]
            new = (
                (diag[row] * value + cw[row] * pltpu.roll(value, 1, 1))
                + (ce[row] * pltpu.roll(value, cols - 1, 1) + up[...] * pltpu.roll(value, levels - 1, 0))
                + down[...] * pltpu.roll(value, 1, 0)
            )
            if row > 0:
                new = new + cs[row] * field[t, row - 1]
            if row < rows - 1:
                new = new + cn[row + 1] * field[t, row + 1]
            if extra is not None:
                new = new + source[extra, row * levels : (row + 1) * levels, :]
            put(out, row, new)
            if out is not None and 0 < row < rows - 1:
                total = pack(total, new, row)
        return total

    def finish(t, out, forward, total, send):
        cw, ce, cs, cn = coefs(forward)
        for copy in row_copies(t) + col_copies(t):
            copy.wait_recv()
        met = jnp.where(
            even, pltpu.roll(edge_col[t, 0], 1, 1), pltpu.roll(edge_col[t, 1], cols - 1, 1)
        )
        gain = (rim_ahead if forward else rim_back) * met
        low = get(out, 0) + cs[0] * edge_row[t, 0]
        high = get(out, rows - 1) + cn[rows] * edge_row[t, 1]
        put(out, 0, low + jnp.where(rim, unpack(gain, 0), 0.0))
        put(out, rows - 1, high + jnp.where(rim, unpack(gain, rows - 1), 0.0))
        if send:
            packed[out] = pack(pack(total, low, 0), high, rows - 1) + gain
            for copy in col_copies(out) + row_copies(out):
                copy.start()
        for row in range(1, rows - 1):
            put(out, row, get(out, row) + jnp.where(rim, unpack(gain, row), 0.0))

    def observe(k, slot, final):
        n_obs = cell_ref.shape[1]
        cell = cell_ref[pl.ds(k, 1), :]
        place = (cell // cols) * levels + level_ref[pl.ds(k, 1), :]
        col = lax.rem(cell, cols)
        cols_hot = lax.broadcasted_iota(jnp.int32, (cols, n_obs), 0) == col
        pick = jnp.where(cols_hot, 1.0, 0.0).astype(jnp.bfloat16)
        pick = jnp.concatenate([pick, pick], 0)
        group = 4 * levels
        spots = lax.broadcasted_iota(jnp.int32, (group, n_obs), 0)

        found = jnp.zeros((8, n_obs), jnp.float32)
        for row in range(0, rows, 4):
            value = field[slot, row : row + 4].reshape(group, cols)
            values = jnp.dot(
                jnp.concatenate(halves(value), 1), pick, preferred_element_type=jnp.float32
            )
            values = jnp.where(spots == place - row * levels, values, 0.0)
            found = found + jnp.sum(values.reshape(group // 8, 8, n_obs), axis=0)
        innovation = jnp.sum(found, axis=0, keepdims=True) - value_ref[pl.ds(k, 1), :]
        weighted = weight_ref[pl.ds(k, 1), :] * innovation
        share = jnp.concatenate(halves(jnp.where(cols_hot, weighted, 0.0)), 0)

        for row in range(0, rows, 4):
            hot = jnp.where(spots == place - row * levels, 1.0, 0.0).astype(jnp.bfloat16)
            both = lax.dot_general(
                hot, share, (((1,), (1,)), ((), ())), preferred_element_type=jnp.float32
            )
            value = both[:, :cols] + both[:, cols:]
            if final:
                field[STEPS + 1, row : row + 4] = value.reshape(4, levels, cols)
            else:
                source[k, row * levels : row * levels + group, :] = value
        return 0.5 * jnp.sum(weighted * innovation, axis=1, keepdims=True)

    cost = jnp.zeros((1, 1), jnp.float32)
    def ahead(k, carry):
        total, cost = carry
        finish(k, k + 1, True, total, True)
        total = inside(k + 1, k + 2, True, None)
        return total, cost + observe(k, k + 1, False)

    total, cost = lax.fori_loop(0, STEPS - 1, ahead, (inside(0, 1, True, None), cost))
    finish(STEPS - 1, STEPS, True, total, False)
    cost = cost + observe(STEPS - 1, STEPS, True)

    for copy in row_copies(STEPS + 1):
        copy.start()
    total = jnp.zeros((fold, cols), jnp.float32)
    for row in range(rows):
        total = pack(total, field[STEPS + 1, row], row)
    packed[STEPS + 1] = total
    for copy in col_copies(STEPS + 1):
        copy.start()

    def spread(mine, board, others, send, recv):
        return [
            remote(board.at[mine], board.at[mine], send.at[d], recv.at[d], other)
            for d, other in enumerate(others)
        ]

    def drain(board, others, send, recv):
        for d, other in enumerate(others):
            copy = remote(board.at[0], board.at[0], send.at[d], recv.at[d], other)
            copy.wait_send()
            copy.wait_recv()

    cost_lon[lo] = jnp.broadcast_to(cost, (8, 128))
    for copy in spread(lo, cost_lon, lon_others, lon_send, lon_recv):
        copy.start()

    def back(k, carry):
        slot = STEPS + 1 + k
        total = inside(slot, slot + 1, False, STEPS - 2 - k)
        finish(slot, slot + 1, False, total, True)
        return carry

    lax.fori_loop(0, STEPS - 1, back, 0)
    drain(cost_lon, lon_others, lon_send, lon_recv)
    cost_lat[la] = jnp.sum(cost_lon[...], axis=0)
    for copy in spread(la, cost_lat, lat_others, lat_send, lat_recv):
        copy.start()
    finish(2 * STEPS, None, False, inside(2 * STEPS, None, False, None), False)
    drain(cost_lat, lat_others, lat_send, lat_recv)
    cost_ref[0, 0] = jnp.sum(cost_lat[...], axis=0)[0, 0]

    for copy in face_copies:
        copy.wait_send()
    for t in [*range(STEPS), *range(STEPS + 1, 2 * STEPS + 1)]:
        for copy in row_copies(t) + col_copies(t):
            copy.wait_send()


def on_device(
    n_lat, n_lon,
    initial, east_wind, north_wind, east_mask, north_mask, mixing,
    obs_cell, obs_level, obs_value, obs_weight,
):
    levels, rows, cols = initial.shape
    n_obs = obs_cell.shape[-1]
    flat = (levels * rows, cols)
    f32 = jnp.float32
    fold = levels * 2 * rows // cols
    vmem = pl.BlockSpec(memory_space=pltpu.VMEM)
    dma = pltpu.SemaphoreType.DMA
    gradient, cost = pl.pallas_call(
        functools.partial(window, n_lat, n_lon, levels, rows, cols),
        out_shape=(jax.ShapeDtypeStruct(flat, f32), jax.ShapeDtypeStruct((1, 1), f32)),
        in_specs=[pl.BlockSpec(memory_space=pl.ANY)] * 10,
        out_specs=(vmem, pl.BlockSpec(memory_space=pltpu.SMEM)),
        scratch_shapes=[
            pltpu.VMEM(flat, f32),
            pltpu.VMEM(flat, f32),
            pltpu.VMEM(flat, f32),
            pltpu.VMEM(flat, jnp.int32),
            pltpu.VMEM(flat, jnp.int32),
            pltpu.SMEM(mixing.shape, f32),
            pltpu.VMEM((STEPS, n_obs), jnp.int32),
            pltpu.VMEM((STEPS, n_obs), jnp.int32),
            pltpu.VMEM((STEPS, n_obs), f32),
            pltpu.VMEM((STEPS, n_obs), f32),
            pltpu.VMEM((2 * STEPS + 1, rows, levels, cols), f32),
            pltpu.VMEM((STEPS - 1,) + flat, f32),
            pltpu.VMEM((rows, levels, cols), f32),
            pltpu.VMEM((rows, levels, cols), f32),
            pltpu.VMEM((rows, levels, cols), f32),
            pltpu.VMEM((rows, levels, cols), f32),
            pltpu.VMEM((rows, levels, cols), f32),
            pltpu.VMEM((rows + 1, levels, cols), f32),
            pltpu.VMEM((rows + 1, levels, cols), f32),
            pltpu.VMEM((levels, cols), f32),
            pltpu.VMEM((levels, cols), f32),
            pltpu.VMEM((2 * STEPS + 1, 2, levels, cols), f32),
            pltpu.VMEM((2 * STEPS + 1, 2, fold, cols), f32),
            pltpu.VMEM((2 * STEPS + 1, fold, cols), f32),
            pltpu.VMEM((fold, cols), f32),
            pltpu.VMEM((fold, cols), f32),
            pltpu.VMEM((n_lon, 8, 128), f32),
            pltpu.VMEM((n_lat, 8, 128), f32),
            dma((2 * STEPS + 1, 4)),
            dma((2 * STEPS + 1, 4)),
            dma((3,)),
            dma((3,)),
            dma((n_lon - 1,)),
            dma((n_lon - 1,)),
            dma((n_lat - 1,)),
            dma((n_lat - 1,)),
            dma((10,)),
        ],
        compiler_params=pltpu.CompilerParams(
            collective_id=0, has_side_effects=True, vmem_limit_bytes=54350 * 1024
        ),
        cost_estimate=pl.CostEstimate(
            flops=8 * 14 * levels * rows * cols, bytes_accessed=24 * levels * rows * cols, transcendentals=0
        ),
    )(
        initial.reshape(flat), east_wind.reshape(flat), north_wind.reshape(flat),
        east_mask.reshape(flat), north_mask.reshape(flat), mixing,
        obs_cell.reshape(STEPS, n_obs), obs_level.reshape(STEPS, n_obs),
        obs_value.reshape(STEPS, n_obs), obs_weight.reshape(STEPS, n_obs),
    )
    return gradient.reshape(levels, rows, cols), cost[0, 0]


def solution(mesh):
    grid = P(None, "lat", "lon")
    spots = P("lat", "lon", None, None)
    return jax.shard_map(
        functools.partial(on_device, mesh.shape["lat"], mesh.shape["lon"]),
        mesh=mesh,
        in_specs=(grid,) * 5 + (P(),) + (spots,) * 4,
        out_specs=(grid, P()),
        check_vma=False,
    )
```
